32 devices in a mesh: grp: 2 (over y), tp: 4 (over z), pd: 4 (over x, core).
Axes of the slice: x: 2, y: 2, z: 4, core: 2. Of those that a mesh axis runs over, the one named last changes fastest.
Arguments:
- x_attn: bfloat16 [2048, 8192], P(('grp', 'pd'), 'tp'), parts along dimension 0, may hold values from -16 to 16
- w_query: bfloat16 [8192, 8192], P(None, 'tp'), may hold values from -0.0625 to 0.0625
- w_keyval: bfloat16 [8192, 2048], replicated, may hold values from -0.0625 to 0.0625
- cache_pool: bfloat16 [8, 64, 16, 2048], P(('grp', 'pd'), 'tp'), parts along dimension 0, may hold values from -8 to 8
- page_table: int32 [8, 64], P(('grp', 'pd')), parts along dimension 0, may hold values from 0 to 63, each once within a row
- cached_len: int32 [8], P(('grp', 'pd')), parts along dimension 0, may hold values from 256 to 1024, as said below
- page_dest: int32 [8, 16, 1], P(('grp', 'pd')), parts along dimension 0, may hold values from 0 to 3; in each aligned block of 16 rows (0 to 15, 16 to 31, ..., all dimensions but the last counted through in order) at most 8 rows name the same one
- mamba_in: bfloat16 [2048, 16384], P(('grp', 'pd'), 'tp'), parts along dimension 0, may hold values from -6 to 6
- gate_in: bfloat16 [2048, 16384], P(('grp', 'pd'), 'tp'), parts along dimension 0, may hold values from -6 to 6
- conv_prev: bfloat16 [8, 3, 16384], P(('grp', 'pd'), None, 'tp'), parts along dimension 0, may hold values from -6 to 6
- state_prev: float32 [8, 16, 16384], P(('grp', 'pd'), None, 'tp'), parts along dimension 0, may hold values from -6 to 6
- conv_weight: float32 [4, 16384], P(None, 'tp'), may hold values from -0.8 to 0.8
- conv_bias: float32 [16384], P('tp'), may hold values from -0.5 to 0.5
- w_xdt: bfloat16 [16384, 512], P('tp'), may hold values from -0.046875 to 0.046875
- w_bc: bfloat16 [16384, 32], P('tp'), may hold values from -0.09375 to 0.09375
- w_dt: bfloat16 [512, 16384], P(None, 'tp'), may hold values from -0.25 to 0.25
- dt_bias: float32 [16384], P('tp'), may hold values from -6 to -1
- a_log: float32 [16, 16384], P(None, 'tp'), may hold values from -3 to 2.8
- d_skip: float32 [16384], P('tp'), may hold values from 0.5 to 1.5
Outputs:
- attn_out: bfloat16 [2048, 8192], P(('grp', 'pd'), 'tp'), parts along dimension 0
- decode_pages: bfloat16 [8, 32, 16, 2048], P(('grp', 'pd'), 'tp'), parts along dimension 0
- mamba_out: bfloat16 [2048, 16384], P(('grp', 'pd'), 'tp'), parts along dimension 0
- final_state: float32 [8, 16, 16384], P(('grp', 'pd'), None, 'tp'), parts along dimension 0
The draws below stay inside these ranges and needn't reach their ends.
There are 2 independent parts, one for each index of `grp`. The reference program is written for one: setup_inputs(seed, part) draws one part's arguments, and reference() takes and returns one part's arrays. A program takes and returns all parts, laid end to end along the dimension named above; an argument that names none is the same for every part. Nothing has to cross between parts.
Inputs may be any that keep to these rules, and one draw needn't show every extreme that they name: `page_table`: row p is a permutation: entry j names the pool slot that holds logical cached page j of prompt p. `cached_len`: some prompt has exactly 1024 cached tokens. `page_dest`: within one prompt no device receives more than 8 new pages, and some device receives exactly 8.
All inputs are finite; a program needn't handle non-finite values.
Results may differ from the reference program's by a relative error of at most 0.017.
Values may be sent and summed in bfloat16 or wider, within the bound.
A program may use at most 512 MiB of HBM per device.

```python
import math
import jax
import jax.numpy as jnp
import numpy as np
from jax import lax

D = 8192
HEADS = 64
KV_HEADS = 8
HEAD_DIM = 128
INNER = 16384
STATE = 16
DT_RANK = 512
CONV = 4
PAGE = 16
NEW_TOKENS = 256
PROMPTS = 4
TOKENS = 1024
CACHE_SLOTS = 64
CACHE_TOK = 1024
NEW_PAGES = 16
MOST = 8
KVCOLS = 2048
N_TP = 4


def draw_x_attn(key, part):
    key = jax.random.fold_in(key, 5)
    leading = jax.random.fold_in(key, 0)
    values = jax.random.normal(leading, (TOKENS, D), jnp.float32)
    return jnp.clip(values, -6.0, 6.0).astype(jnp.bfloat16)


def draw_cache_pool(key, part):
    key = jax.random.fold_in(key, 7)
    values = jax.random.normal(key, (PROMPTS, CACHE_SLOTS, PAGE, KVCOLS), jnp.float32)
    return jnp.clip(values, -6.0, 6.0).astype(jnp.bfloat16)


def draw_cached_len(key, part):
    key = jax.random.fold_in(key, 11)
    leading, second = jax.random.split(key)
    lengths = jax.random.randint(leading, (PROMPTS,), CACHE_TOK // 4, CACHE_TOK + 1)
    longest = jax.random.randint(second, (), 0, PROMPTS)
    return jnp.where(jnp.arange(PROMPTS) == longest, CACHE_TOK, lengths).astype(jnp.int32)


def level_of(stream_key, extent, cuts, smallest, top_value):
    loudness = 1.0
    for axis_at, parts in cuts:
        draws = jax.random.uniform(jax.random.fold_in(jax.random.fold_in(stream_key, 6), axis_at), (parts,), jnp.float32, smallest / len(cuts), top_value / len(cuts))
        loudness = loudness * jnp.repeat(jnp.exp(draws), extent[axis_at] // parts).reshape((-1,) + (1,) * (len(extent) - 1 - axis_at))
    return loudness


def assign_block(key, own, number, rows, count, top, bound, lean):
    order = jax.random.permutation(key, count)
    heavy_load, ordinary = portions_of(count, rows * top, bound, lean, True), portions_of(count, rows * top, bound, lean, False)
    places = jnp.arange(count)

    def named(sizes, rotation):
        used = int((sizes > 0).sum())
        fixed = max(1, used // 4)
        moved = fixed + (places - fixed + rotation * (used - fixed)) % max(1, count - fixed)
        return jnp.zeros((count,), jnp.int32).at[order[jnp.where(places < fixed, places, moved)]].set(jnp.asarray(sizes, jnp.int32))

    sizes = jnp.where(number % 4 == 0, named(heavy_load, number // 4), named(ordinary, number - number // 4 - 1))
    mixed = jax.random.permutation(jax.random.fold_in(own, 3), count)
    giver, receiver = mixed[0:count // 2 * 2:2], mixed[1:count // 2 * 2:2]
    margin = jnp.minimum(sizes[giver] - 1, bound - sizes[receiver]) // 2
    margin = jnp.where((giver == order[0]) | (receiver == order[0]) | (sizes[receiver] == 0), 0, jnp.maximum(margin, 0))
    moved = jax.random.randint(jax.random.fold_in(own, 4), (count // 2,), 0, 1 << 20) % (margin + 1)
    sizes = sizes.at[giver].add(-moved).at[receiver].add(moved)
    labels = jnp.searchsorted(jnp.cumsum(sizes), jnp.arange(rows * top), side="right").astype(jnp.int32)
    table = labels.reshape(top, rows).T
    table = table[jax.random.permutation(jax.random.fold_in(own, 1), rows)]
    rotation = jax.random.randint(jax.random.fold_in(own, 2), (rows, 1), 0, top)
    return jnp.take_along_axis(table, (jnp.arange(top)[None, :] + rotation) % top, axis=1)


def portions_of(number_of, total, most, skew, full):
    loads = [(1 << 20) // math.isqrt(standing ** skew) + 1 for standing in range(1, number_of + 1)]
    largest = most if full else min(most, max(-(-total // number_of), total * loads[0] // sum(loads)))
    least = 1 if total - largest >= number_of - 1 else 0
    holding, surplus = [largest] + [least] * (number_of - 1), total - largest - least * (number_of - 1)
    while surplus > 0:
        movable = [i for i in range(1, number_of) if holding[i] < largest] or [i for i in range(1, number_of) if holding[i] < most]
        pool, left = sum([loads[i] for i in movable]), surplus
        for i in movable:
            extra = min(most - holding[i], max(1, left * loads[i] // pool), surplus)
            holding[i] = holding[i] + extra
            surplus = surplus - extra
    return np.array(holding)


def bell_draw(own_key, shape, spread, bound, cuts=(), held_as=jnp.bfloat16):
    drawn = jax.random.normal(own_key, shape, jnp.float32) * spread
    if len(cuts) > 0:
        drawn = level_of(own_key, shape, cuts, -0.22, 0.18) * drawn
    return jnp.clip(drawn, min=-bound, max=bound).astype(held_as)


def setup_inputs(seed: int = 0, part: int = 0) -> dict:
    keys = jax.random.split(jax.random.key(seed), 20)
    part_splits = jax.random.split(jax.random.fold_in(keys[19], part), 20)
    x_attn = draw_x_attn(jax.random.fold_in(jax.random.fold_in(keys[19], part), 71), part)
    w_query = bell_draw(keys[1], (D, HEADS * HEAD_DIM), D ** -0.5, 0.0625, ((1, 4),))
    w_keyval = bell_draw(keys[2], (D, KVCOLS), D ** -0.5, 0.0625)
    cache_pool = draw_cache_pool(jax.random.fold_in(jax.random.fold_in(keys[19], part), 71), part)
    page_table = jax.vmap(lambda own: jax.random.permutation(own, CACHE_SLOTS))(jax.random.split(part_splits[4], PROMPTS)).reshape((PROMPTS, CACHE_SLOTS)).astype(jnp.int32)
    cached_len = draw_cached_len(jax.random.fold_in(jax.random.fold_in(keys[19], part), 71), part)
    page_dest_keys = jax.random.split(jax.random.fold_in(part_splits[6], 1), PROMPTS * NEW_PAGES // NEW_PAGES)
    page_dest_turns = jax.random.permutation(jax.random.fold_in(part_splits[6], 3), PROMPTS * NEW_PAGES // NEW_PAGES)
    page_dest = jax.vmap(lambda own, number: assign_block(jax.random.fold_in(part_splits[6], 2), own, number, NEW_PAGES, N_TP, 1, MOST, 2))(page_dest_keys, page_dest_turns).reshape((PROMPTS, NEW_PAGES, 1))
    mamba_in = bell_draw(part_splits[7], (TOKENS, INNER), 1.0, 6.0, ((0, 4), (1, 4)))
    gate_in = bell_draw(part_splits[8], (TOKENS, INNER), 1.0, 6.0, ((0, 4), (1, 4)))
    conv_prev = bell_draw(part_splits[9], (PROMPTS, CONV - 1, INNER), 1.0, 6.0, ((0, 4), (2, 4)))
    state_prev = bell_draw(part_splits[10], (PROMPTS, STATE, INNER), 1.0, 6.0, ((0, 4), (2, 4)), jnp.float32)
    conv_weight = jnp.clip(jax.random.uniform(keys[11], (CONV, INNER), jnp.float32, -0.8, 0.8) * level_of(keys[11], (CONV, INNER), ((1, 4),), -0.4, 0.0), -0.8, 0.8)
    conv_bias = jnp.clip(jax.random.uniform(keys[12], (INNER,), jnp.float32, -0.5, 0.5) * level_of(keys[12], (INNER,), ((0, 4),), -0.4, 0.0), -0.5, 0.5)
    w_xdt = bell_draw(keys[13], (INNER, DT_RANK), INNER ** -0.5, 0.046875, ((0, 4),))
    w_bc = bell_draw(keys[14], (INNER, 2 * STATE), (INNER // 4) ** -0.5, 0.09375, ((0, 4),))
    w_dt = bell_draw(keys[15], (DT_RANK, INNER), DT_RANK ** -0.5, 0.25, ((1, 4),))
    dt_bias = jnp.clip(-6.0 + 5.0 * jax.random.uniform(keys[16], (INNER,), jnp.float32) ** level_of(keys[16], (INNER,), ((0, 4),), -0.2, 0.2), -6.0, -1.0)
    a_log = jnp.clip(-3.0 + 5.8 * jax.random.uniform(keys[17], (STATE, INNER), jnp.float32) ** level_of(keys[17], (STATE, INNER), ((1, 4),), -0.2, 0.2), -3.0, 2.8)
    d_skip = jnp.clip(0.5 + 1.0 * jax.random.uniform(keys[18], (INNER,), jnp.float32) ** level_of(keys[18], (INNER,), ((0, 4),), -0.2, 0.2), 0.5, 1.5)
    return {"x_attn": x_attn, "w_query": w_query, "w_keyval": w_keyval, "cache_pool": cache_pool, "page_table": page_table, "cached_len": cached_len, "page_dest": page_dest, "mamba_in": mamba_in, "gate_in": gate_in, "conv_prev": conv_prev, "state_prev": state_prev, "conv_weight": conv_weight, "conv_bias": conv_bias, "w_xdt": w_xdt, "w_bc": w_bc, "w_dt": w_dt, "dt_bias": dt_bias, "a_log": a_log, "d_skip": d_skip}


def prompt_attention(hidden, page_map, length, page_pool, page_target, w_query, w_keyval):
    queries = jnp.dot(hidden, w_query, preferred_element_type=jnp.float32).astype(jnp.bfloat16)
    keyvals = jnp.dot(hidden, w_keyval, preferred_element_type=jnp.float32).astype(jnp.bfloat16)
    slot_count = page_map.shape[0]
    slot_page = jnp.zeros((slot_count,), jnp.int32).at[page_map].set(jnp.arange(slot_count, dtype=jnp.int32))
    positions = slot_page[:, None] * PAGE + jnp.arange(PAGE, dtype=jnp.int32)[None, :]
    cache_usable = (positions < length).reshape(-1)
    token_count = hidden.shape[0]
    token_ids = jnp.arange(token_count, dtype=jnp.int32)
    causal = token_ids[:, None] >= token_ids[None, :]
    usable = jnp.concatenate([jnp.broadcast_to(cache_usable[None, :], (token_count, cache_usable.shape[0])), causal], axis=1)
    group_size = HEADS // KV_HEADS
    pool_heads = page_pool.reshape(slot_count * PAGE, KV_HEADS, 2, HEAD_DIM)
    new_heads = keyvals.reshape(token_count, KV_HEADS, 2, HEAD_DIM)
    key_heads = jnp.moveaxis(jnp.concatenate([pool_heads[:, :, 0], new_heads[:, :, 0]], axis=0), 1, 0)
    value_heads = jnp.moveaxis(jnp.concatenate([pool_heads[:, :, 1], new_heads[:, :, 1]], axis=0), 1, 0)
    query_heads = jnp.moveaxis(queries.reshape(token_count, KV_HEADS, group_size, HEAD_DIM), 1, 0)

    def per_head(operands):
        query_head, key_head, value_head = operands
        scores = jnp.einsum('cgd,ld->cgl', query_head.astype(jnp.float32), key_head.astype(jnp.float32)) / math.sqrt(HEAD_DIM)
        scores = jnp.where(usable[:, None, :], scores, -jnp.inf)
        highest = lax.optimization_barrier(jnp.max(scores, axis=-1, keepdims=True))
        weights = jnp.exp(scores - highest)
        totals = lax.optimization_barrier(jnp.sum(weights, axis=-1))
        probs = weights.astype(jnp.bfloat16)
        mixture = jnp.einsum('cgl,ld->cgd', probs.astype(jnp.float32), value_head.astype(jnp.float32))
        return (mixture / totals[..., None]).astype(jnp.bfloat16)
    heads_out = lax.map(per_head, (query_heads, key_heads, value_heads))
    attended = jnp.moveaxis(heads_out, 0, 1).reshape(token_count, HEADS * HEAD_DIM)
    page_count = token_count // PAGE
    new_pages = keyvals.reshape(page_count, PAGE * KVCOLS)
    target = page_target[:, 0]
    page_ids = jnp.arange(page_count, dtype=jnp.int32)
    earlier = (target[None, :] == target[:, None]) & (page_ids[None, :] < page_ids[:, None])
    ranking = lax.optimization_barrier(jnp.sum(earlier.astype(jnp.int32), axis=1))
    position = target * MOST + ranking
    decode = jnp.zeros((N_TP * MOST, PAGE * KVCOLS), jnp.bfloat16).at[position].set(new_pages)
    return (attended, decode.reshape(N_TP * MOST, PAGE, KVCOLS))

def prompt_mamba(mamba_rows, gate_rows, previous, initial, conv_weight, conv_bias, w_xdt, w_bc, w_dt, dt_bias, a_log, d_skip):
    token_count = mamba_rows.shape[0]
    extended = jnp.concatenate([previous, mamba_rows], axis=0).astype(jnp.float32)
    convolved = jnp.broadcast_to(conv_bias[None, :], (token_count, conv_bias.shape[0])).astype(jnp.float32)
    for offset in range(CONV):
        convolved = convolved + conv_weight[offset][None, :] * extended[offset:offset + token_count]
    xconv = jax.nn.silu(convolved).astype(jnp.bfloat16)
    projected = jnp.dot(xconv, w_xdt, preferred_element_type=jnp.float32)
    selection = jnp.dot(xconv, w_bc, preferred_element_type=jnp.float32)
    low_norm = (projected * lax.rsqrt(lax.optimization_barrier(jnp.mean(projected * projected, axis=-1, keepdims=True)) + 1e-06)).astype(jnp.bfloat16)
    step_size = jax.nn.softplus(jnp.dot(low_norm, w_dt, preferred_element_type=jnp.float32) + dt_bias[None, :])
    decay_rate = -jnp.exp(a_log)
    xconv_f = xconv.astype(jnp.float32)

    def advance(state, inputs):
        step_row, input_row, read_row, x_row = inputs
        state = jnp.exp(step_row[None, :] * decay_rate) * state + (step_row * x_row)[None, :] * input_row[:, None]
        output = lax.optimization_barrier(jnp.sum(read_row[:, None] * state, axis=0)) + d_skip * x_row
        return (state, output)
    last_state, outputs = lax.scan(advance, initial, (step_size, selection[:, :STATE], selection[:, STATE:], xconv_f))
    gated = (outputs * jax.nn.silu(gate_rows.astype(jnp.float32))).astype(jnp.bfloat16)
    return (gated, last_state)

def reference(x_attn, w_query, w_keyval, cache_pool, page_table, cached_len, page_dest, mamba_in, gate_in, conv_prev, state_prev, conv_weight, conv_bias, w_xdt, w_bc, w_dt, dt_bias, a_log, d_skip):
    hidden = x_attn.reshape(PROMPTS, NEW_TOKENS, D)

    def attention_one(operands):
        return prompt_attention(operands[0], operands[1], operands[2], operands[3], operands[4], w_query, w_keyval)
    attended, decode = lax.map(attention_one, (hidden, page_table, cached_len, cache_pool, page_dest))

    def mamba_one(operands):
        return prompt_mamba(operands[0], operands[1], operands[2], operands[3], conv_weight, conv_bias, w_xdt, w_bc, w_dt, dt_bias, a_log, d_skip)
    gated, last_state = lax.map(mamba_one, (mamba_in.reshape(PROMPTS, NEW_TOKENS, INNER), gate_in.reshape(PROMPTS, NEW_TOKENS, INNER), conv_prev, state_prev))
    return (attended.reshape(PROMPTS * NEW_TOKENS, HEADS * HEAD_DIM), decode, gated.reshape(PROMPTS * NEW_TOKENS, INNER), last_state)
```

```python
import functools
import math

import jax
import jax.numpy as jnp
from jax import lax
from jax.experimental import pallas as pl
from jax.experimental.pallas import tpu as pltpu
from jax.sharding import PartitionSpec as P

HEADS = 64
KV_HEADS = 8
HEAD_DIM = 128
PAGE = 16
MASKED = -1e30
LOG2E = math.log2(math.e)
MIB = 1024 * 1024


def token_usable(page_map, slot_ids, length):
    logical = jnp.sum(
        jnp.where(
            page_map[None, :] == slot_ids[:, None], jnp.arange(page_map.shape[0])[None, :], 0
        ),
        axis=1,
    )
    positions = logical[:, None] * PAGE + jnp.arange(PAGE)[None, :]
    return (positions < length).reshape(-1)


def attention_kernel(chunk, bias_ref, query_ref, cached_ref, fresh_ref, out_ref):
    tokens = query_ref.shape[0]
    query = query_ref[...]
    scale = LOG2E / math.sqrt(HEAD_DIM)
    contract = (((1,), (1,)), ((), ()))

    def scored(keys):
        return lax.dot_general(query, keys, contract, preferred_element_type=jnp.float32) * scale

    rows = lax.broadcasted_iota(jnp.int32, (tokens, tokens), 0)
    cols = lax.broadcasted_iota(jnp.int32, (tokens, tokens), 1)
    near = jnp.where(rows >= cols, scored(fresh_ref[:, :HEAD_DIM]), MASKED)
    near_high = jnp.max(near, axis=1, keepdims=True)

    def mix(weights, values):
        return jnp.dot(
            weights.astype(jnp.bfloat16), values, preferred_element_type=jnp.float32
        )

    chunks = cached_ref.shape[0] // chunk
    if chunks == 1:
        far = scored(cached_ref[:, :HEAD_DIM]) + bias_ref[...]
        high = jnp.maximum(near_high, jnp.max(far, axis=1, keepdims=True))
        near_w = jnp.exp2(near - high)
        far_w = jnp.exp2(far - high)
        total = jnp.sum(near_w, axis=1, keepdims=True) + jnp.sum(far_w, axis=1, keepdims=True)
        mixture = mix(near_w, fresh_ref[:, HEAD_DIM:]) + mix(far_w, cached_ref[:, HEAD_DIM:])
        out_ref[...] = (mixture / total).astype(out_ref.dtype)
        return
    near_w = jnp.exp2(near - near_high)
    start = (
        near_high,
        jnp.sum(near_w, axis=1, keepdims=True),
        mix(near_w, fresh_ref[:, HEAD_DIM:]),
    )

    def step(i, carry):
        high, total, mixture = carry
        here = pl.ds(pl.multiple_of(i * chunk, chunk), chunk)
        far = scored(cached_ref[here, :HEAD_DIM]) + bias_ref[:, here]
        peak = jnp.maximum(high, jnp.max(far, axis=1, keepdims=True))
        far_w = jnp.exp2(far - peak)
        shrink = jnp.exp2(high - peak)
        return (
            peak,
            total * shrink + jnp.sum(far_w, axis=1, keepdims=True),
            mixture * shrink + mix(far_w, cached_ref[here, HEAD_DIM:]),
        )

    _, total, mixture = lax.fori_loop(0, chunks, step, start)
    out_ref[...] = (mixture / total).astype(out_ref.dtype)


def attend(queries, cached, fresh, bias, own_groups, per_group):
    tokens = queries.shape[0]
    length = cached.shape[0]
    chunk = min(1024, length)
    return pl.pallas_call(
        functools.partial(attention_kernel, chunk),
        grid=(own_groups, per_group),
        out_shape=jax.ShapeDtypeStruct(queries.shape, jnp.bfloat16),
        in_specs=[
            pl.BlockSpec((1, length), lambda g, h: (0, 0)),
            pl.BlockSpec((tokens, HEAD_DIM), lambda g, h: (0, g * per_group + h)),
            pl.BlockSpec((length, 2 * HEAD_DIM), lambda g, h: (0, g)),
            pl.BlockSpec((tokens, 2 * HEAD_DIM), lambda g, h: (0, g)),
        ],
        out_specs=pl.BlockSpec((tokens, HEAD_DIM), lambda g, h: (0, g * per_group + h)),
        compiler_params=pltpu.CompilerParams(vmem_limit_bytes=40 * MIB),
        cost_estimate=pl.CostEstimate(
            flops=4 * tokens * queries.shape[1] * (length + tokens),
            bytes_accessed=4 * queries.size + 2 * cached.size,
            transcendentals=tokens * own_groups * per_group * (length + tokens),
        ),
    )(bias, queries, cached, fresh)


def scan_kernel(
    norm_ref, spread_ref, wdt_ref, bias_ref, xconv_ref, gate_ref, alog_ref, skip_ref, init_ref,
    out_ref, final_ref, step_s, push_s, read_s,
):
    tokens, width = xconv_ref.shape
    states = alog_ref.shape[0]
    raw = jnp.dot(norm_ref[...], wdt_ref[...], preferred_element_type=jnp.float32) + bias_ref[...]
    step_size = jnp.maximum(raw, 0.0) + jnp.log1p(jnp.exp(-jnp.abs(raw)))
    step_s[...] = step_size
    push_s[...] = step_size * xconv_ref[...].astype(jnp.float32)
    rate = jnp.exp(alog_ref[...]) * (-LOG2E)
    unroll = 8

    def some(block, state):
        base = pl.multiple_of(block * unroll, unroll)
        for i in range(unroll):
            here = pl.ds(base + i, 1)
            step_row = jnp.broadcast_to(step_s[here, :], (states, width))
            push_row = jnp.broadcast_to(push_s[here, :], (states, width))
            columns = spread_ref[base + i]
            into = jnp.concatenate([columns[:states]] * (width // 128), axis=1)
            outof = jnp.concatenate([columns[states:]] * (width // 128), axis=1)
            state = jnp.exp2(step_row * rate) * state + push_row * into
            read_s[here, :] = jnp.sum(outof * state, axis=0, keepdims=True)
        return state

    final_ref[...] = lax.fori_loop(0, tokens // unroll, some, init_ref[...])
    readout = read_s[...] + skip_ref[...] * xconv_ref[...].astype(jnp.float32)
    gate = gate_ref[...].astype(jnp.float32)
    out_ref[...] = (readout * (gate * jax.nn.sigmoid(gate))).astype(out_ref.dtype)


def scan(low_norm, selection, w_dt, dt_bias, xconv, gate, a_log, d_skip, initial):
    tokens, channels = xconv.shape
    rank = low_norm.shape[1]
    states = a_log.shape[0]
    width = min(512, channels)
    spread = jnp.broadcast_to(selection[:, :, None], (tokens, 2 * states, 128))

    def whole(shape):
        return pl.BlockSpec(shape, lambda c: (0,) * len(shape))

    def columns(rows):
        return pl.BlockSpec((rows, width), lambda c: (0, c))

    return pl.pallas_call(
        scan_kernel,
        grid=(channels // width,),
        out_shape=(
            jax.ShapeDtypeStruct((tokens, channels), jnp.bfloat16),
            jax.ShapeDtypeStruct((states, channels), jnp.float32),
        ),
        in_specs=[
            whole((tokens, rank)),
            whole((tokens, 2 * states, 128)),
            columns(rank),
            columns(1),
            columns(tokens),
            columns(tokens),
            columns(states),
            columns(1),
            columns(states),
        ],
        out_specs=(columns(tokens), columns(states)),
        scratch_shapes=[pltpu.VMEM((tokens, width), jnp.float32)] * 3,
        compiler_params=pltpu.CompilerParams(vmem_limit_bytes=40 * MIB),
        cost_estimate=pl.CostEstimate(
            flops=2 * tokens * channels * rank + 7 * tokens * channels * states,
            bytes_accessed=6 * tokens * channels + 2 * rank * channels + 12 * states * channels,
            transcendentals=tokens * channels * states,
        ),
    )(
        low_norm, spread, w_dt, dt_bias[None, :], xconv, gate, a_log, d_skip[None, :], initial
    )


def body(
    x_attn,
    w_query,
    w_keyval,
    cache_pool,
    page_table,
    cached_len,
    page_dest,
    mamba_in,
    gate_in,
    conv_prev,
    state_prev,
    conv_weight,
    conv_bias,
    w_xdt,
    w_bc,
    w_dt,
    dt_bias,
    a_log,
    d_skip,
):
    tp_size = lax.axis_size("tp")
    tp_index = lax.axis_index("tp")
    token_count = x_attn.shape[0]
    own_heads = w_query.shape[1] // HEAD_DIM
    group_size = HEADS // KV_HEADS
    own_groups = max(1, own_heads // group_size)
    per_group = own_heads // own_groups
    head_cols = 2 * HEAD_DIM
    kv_cols = w_keyval.shape[1]
    slice_cols = kv_cols // tp_size
    first_group = tp_index * own_heads // group_size

    extended = jnp.concatenate([conv_prev[0], mamba_in], axis=0).astype(jnp.float32)
    convolved = jnp.broadcast_to(conv_bias[None, :], mamba_in.shape)
    for offset in range(conv_weight.shape[0]):
        convolved = (
            convolved + conv_weight[offset][None, :] * extended[offset : offset + token_count]
        )
    xconv = jax.nn.silu(convolved).astype(jnp.bfloat16)
    proj_part = jnp.dot(xconv, w_xdt, preferred_element_type=jnp.float32)
    select_part = jnp.dot(xconv, w_bc, preferred_element_type=jnp.float32)
    rank = w_xdt.shape[1]
    summed = lax.psum(
        jnp.concatenate([proj_part, select_part], axis=1).astype(jnp.bfloat16), "tp"
    ).astype(jnp.float32)
    projected, selection = summed[:, :rank], summed[:, rank:]

    local_slots = cache_pool.shape[1]
    pool = cache_pool[0].reshape(local_slots * PAGE, KV_HEADS, head_cols)
    if own_heads >= group_size:
        outgoing_kv = pool.reshape(local_slots * PAGE, tp_size, own_groups * head_cols)
    else:
        outgoing_kv = jnp.repeat(pool, group_size // own_heads, axis=1)
    outgoing_kv = jnp.moveaxis(outgoing_kv, 1, 0)
    cached = lax.all_to_all(outgoing_kv, "tp", split_axis=0, concat_axis=0, tiled=True)
    cached = cached.reshape(tp_size * local_slots * PAGE, own_groups * head_cols)
    usable = token_usable(page_table[0], jnp.arange(page_table.shape[1]), cached_len[0])
    bias = jnp.where(usable, 0.0, MASKED).astype(jnp.float32)[None, :]

    w_own = lax.dynamic_slice_in_dim(w_keyval, first_group * head_cols, own_groups * head_cols, 1)
    piece = lax.all_gather(x_attn, "tp", axis=1, tiled=True)
    low_norm = (
        projected * lax.rsqrt(jnp.mean(projected * projected, axis=-1, keepdims=True) + 1e-06)
    ).astype(jnp.bfloat16)
    mamba_out, last_state = scan(
        low_norm, selection, w_dt, dt_bias, xconv, gate_in, a_log, d_skip, state_prev[0]
    )

    fresh = jnp.dot(piece, w_own, preferred_element_type=jnp.float32).astype(jnp.bfloat16)
    queries = jnp.dot(piece, w_query, preferred_element_type=jnp.float32).astype(jnp.bfloat16)

    page_count = token_count // PAGE
    capacity = max(2, 2 * page_count // tp_size)
    target = page_dest[0, :, 0]
    page_ids = jnp.arange(page_count)
    earlier = (target[None, :] == target[:, None]) & (page_ids[None, :] < page_ids[:, None])
    ranking = jnp.sum(earlier.astype(jnp.int32), axis=1)
    slot_ids = jnp.arange(capacity)
    my_slice = lax.dynamic_slice_in_dim(
        fresh, tp_index * slice_cols - first_group * head_cols, slice_cols, 1
    )
    pieces_out = my_slice.reshape(page_count, PAGE * slice_cols)
    onehot = (
        (target[None, None, :] == jnp.arange(tp_size)[:, None, None])
        & (ranking[None, None, :] == slot_ids[None, :, None])
    ).astype(jnp.bfloat16)
    outgoing = jnp.einsum(
        "drj,jx->drx", onehot, pieces_out, preferred_element_type=jnp.float32
    ).astype(jnp.bfloat16)
    arrived = lax.all_to_all(outgoing, "tp", split_axis=0, concat_axis=2, tiled=True)
    decode = (
        arrived.reshape(capacity, tp_size, PAGE, slice_cols)
        .transpose(0, 2, 1, 3)
        .reshape(1, capacity, PAGE, kv_cols)
    )
    attn_out = attend(queries, cached, fresh, bias, own_groups, per_group)
    return (attn_out, decode, mamba_out, last_state[None])


def solution(mesh):
    return jax.shard_map(
        body,
        mesh=mesh,
        in_specs=(
            P(("grp", "pd"), "tp"),
            P(None, "tp"),
            P(),
            P(("grp", "pd"), "tp", None, None),
            P(("grp", "pd"), None),
            P(("grp", "pd")),
            P(("grp", "pd"), None, None),
            P(("grp", "pd"), "tp"),
            P(("grp", "pd"), "tp"),
            P(("grp", "pd"), None, "tp"),
            P(("grp", "pd"), None, "tp"),
            P(None, "tp"),
            P("tp"),
            P("tp", None),
            P("tp", None),
            P(None, "tp"),
            P("tp"),
            P(None, "tp"),
            P("tp"),
        ),
        out_specs=(
            P(("grp", "pd"), "tp"),
            P(("grp", "pd"), "tp", None, None),
            P(("grp", "pd"), "tp"),
            P(("grp", "pd"), None, "tp"),
        ),
        check_vma=False,
    )
```

```python
import functools
import math

import jax
import jax.numpy as jnp
from jax import lax
from jax.experimental import pallas as pl
from jax.experimental.pallas import tpu as pltpu
from jax.sharding import PartitionSpec as P

HEADS = 64
KV_HEADS = 8
HEAD_DIM = 128
PAGE = 16
MASKED = -1e30
LOG2E = math.log2(math.e)
MIB = 1024 * 1024


def token_usable(page_map, slot_ids, length):
    logical = jnp.sum(
        jnp.where(
            page_map[None, :] == slot_ids[:, None], jnp.arange(page_map.shape[0])[None, :], 0
        ),
        axis=1,
    )
    positions = logical[:, None] * PAGE + jnp.arange(PAGE)[None, :]
    return (positions < length).reshape(-1)


def attention_kernel(chunk, bias_ref, query_ref, cached_ref, fresh_ref, out_ref):
    tokens = query_ref.shape[0]
    query = query_ref[...]
    scale = LOG2E / math.sqrt(HEAD_DIM)
    contract = (((1,), (1,)), ((), ()))

    def scored(keys):
        return lax.dot_general(query, keys, contract, preferred_element_type=jnp.float32) * scale

    rows = lax.broadcasted_iota(jnp.int32, (tokens, tokens), 0)
    cols = lax.broadcasted_iota(jnp.int32, (tokens, tokens), 1)
    near = jnp.where(rows >= cols, scored(fresh_ref[:, :HEAD_DIM]), MASKED)
    near_high = jnp.max(near, axis=1, keepdims=True)

    def mix(weights, values):
        return jnp.dot(
            weights.astype(jnp.bfloat16), values, preferred_element_type=jnp.float32
        )

    chunks = cached_ref.shape[0] // chunk
    if chunks == 1:
        far = scored(cached_ref[:, :HEAD_DIM]) + bias_ref[...]
        high = jnp.maximum(near_high, jnp.max(far, axis=1, keepdims=True))
        near_w = jnp.exp2(near - high)
        far_w = jnp.exp2(far - high)
        total = jnp.sum(near_w, axis=1, keepdims=True) + jnp.sum(far_w, axis=1, keepdims=True)
        mixture = mix(near_w, fresh_ref[:, HEAD_DIM:]) + mix(far_w, cached_ref[:, HEAD_DIM:])
        out_ref[...] = (mixture / total).astype(out_ref.dtype)
        return
    near_w = jnp.exp2(near - near_high)
    start = (
        near_high,
        jnp.sum(near_w, axis=1, keepdims=True),
        mix(near_w, fresh_ref[:, HEAD_DIM:]),
    )

    def step(i, carry):
        high, total, mixture = carry
        here = pl.ds(pl.multiple_of(i * chunk, chunk), chunk)
        far = scored(cached_ref[here, :HEAD_DIM]) + bias_ref[:, here]
        peak = jnp.maximum(high, jnp.max(far, axis=1, keepdims=True))
        far_w = jnp.exp2(far - peak)
        shrink = jnp.exp2(high - peak)
        return (
            peak,
            total * shrink + jnp.sum(far_w, axis=1, keepdims=True),
            mixture * shrink + mix(far_w, cached_ref[here, HEAD_DIM:]),
        )

    _, total, mixture = lax.fori_loop(0, chunks, step, start)
    out_ref[...] = (mixture / total).astype(out_ref.dtype)


def attend(queries, cached, fresh, bias, own_groups, per_group):
    tokens = queries.shape[0]
    length = cached.shape[0]
    chunk = min(1024, length)
    return pl.pallas_call(
        functools.partial(attention_kernel, chunk),
        grid=(own_groups, per_group),
        out_shape=jax.ShapeDtypeStruct(queries.shape, jnp.bfloat16),
        in_specs=[
            pl.BlockSpec((1, length), lambda g, h: (0, 0)),
            pl.BlockSpec((tokens, HEAD_DIM), lambda g, h: (0, g * per_group + h)),
            pl.BlockSpec((length, 2 * HEAD_DIM), lambda g, h: (0, g)),
            pl.BlockSpec((tokens, 2 * HEAD_DIM), lambda g, h: (0, g)),
        ],
        out_specs=pl.BlockSpec((tokens, HEAD_DIM), lambda g, h: (0, g * per_group + h)),
        compiler_params=pltpu.CompilerParams(vmem_limit_bytes=40 * MIB),
        cost_estimate=pl.CostEstimate(
            flops=4 * tokens * queries.shape[1] * (length + tokens),
            bytes_accessed=4 * queries.size + 2 * cached.size,
            transcendentals=tokens * own_groups * per_group * (length + tokens),
        ),
    )(bias, queries, cached, fresh)


def scan_kernel(
    norm_ref, spread_ref, wdt_ref, bias_ref, xconv_ref, gate_ref, alog_ref, skip_ref, init_ref,
    out_ref, final_ref, step_s, push_s, read_s,
):
    tokens, width = xconv_ref.shape
    states = alog_ref.shape[0]
    raw = jnp.dot(norm_ref[...], wdt_ref[...], preferred_element_type=jnp.float32) + bias_ref[...]
    step_size = jnp.maximum(raw, 0.0) + jnp.log1p(jnp.exp(-jnp.abs(raw)))
    step_s[...] = step_size
    push_s[...] = step_size * xconv_ref[...].astype(jnp.float32)
    rate = jnp.exp(alog_ref[...]) * (-LOG2E)
    unroll = 8

    def some(block, state):
        base = pl.multiple_of(block * unroll, unroll)
        for i in range(unroll):
            here = pl.ds(base + i, 1)
            step_row = jnp.broadcast_to(step_s[here, :], (states, width))
            push_row = jnp.broadcast_to(push_s[here, :], (states, width))
            columns = spread_ref[base + i]
            into = jnp.concatenate([columns[:states]] * (width // 128), axis=1)
            outof = jnp.concatenate([columns[states:]] * (width // 128), axis=1)
            state = jnp.exp2(step_row * rate) * state + push_row * into
            read_s[here, :] = jnp.sum(outof * state, axis=0, keepdims=True)
        return state

    final_ref[...] = lax.fori_loop(0, tokens // unroll, some, init_ref[...])
    readout = read_s[...] + skip_ref[...] * xconv_ref[...].astype(jnp.float32)
    gate = gate_ref[...].astype(jnp.float32)
    out_ref[...] = (readout * (gate * jax.nn.sigmoid(gate))).astype(out_ref.dtype)


def scan(low_norm, selection, w_dt, dt_bias, xconv, gate, a_log, d_skip, initial):
    tokens, channels = xconv.shape
    rank = low_norm.shape[1]
    states = a_log.shape[0]
    width = min(512, channels)
    spread = jnp.broadcast_to(selection[:, :, None], (tokens, 2 * states, 128))

    def whole(shape):
        return pl.BlockSpec(shape, lambda c: (0,) * len(shape))

    def columns(rows):
        return pl.BlockSpec((rows, width), lambda c: (0, c))

    return pl.pallas_call(
        scan_kernel,
        grid=(channels // width,),
        out_shape=(
            jax.ShapeDtypeStruct((tokens, channels), jnp.bfloat16),
            jax.ShapeDtypeStruct((states, channels), jnp.float32),
        ),
        in_specs=[
            whole((tokens, rank)),
            whole((tokens, 2 * states, 128)),
            columns(rank),
            columns(1),
            columns(tokens),
            columns(tokens),
            columns(states),
            columns(1),
            columns(states),
        ],
        out_specs=(columns(tokens), columns(states)),
        scratch_shapes=[pltpu.VMEM((tokens, width), jnp.float32)] * 3,
        compiler_params=pltpu.CompilerParams(vmem_limit_bytes=40 * MIB),
        cost_estimate=pl.CostEstimate(
            flops=2 * tokens * channels * rank + 7 * tokens * channels * states,
            bytes_accessed=6 * tokens * channels + 2 * rank * channels + 12 * states * channels,
            transcendentals=tokens * channels * states,
        ),
    )(
        low_norm, spread, w_dt, dt_bias[None, :], xconv, gate, a_log, d_skip[None, :], initial
    )


def project_kernel(count, has_sum, where_ref, *refs):
    pieces, weight_ref = refs[:count], refs[count]
    out_ref, total = refs[-2], refs[-1]
    at = pl.program_id(1)

    @pl.when(at == 0)
    def _():
        total[...] = refs[count + 1][...] if has_sum else jnp.zeros_like(total)

    for i in range(count):

        @pl.when(at == i)
        def _(i=i):
            total[...] += jnp.dot(
                pieces[i][...], weight_ref[...], preferred_element_type=jnp.float32
            )

    @pl.when(at == count - 1)
    def _():
        out_ref[...] = total[...].astype(out_ref.dtype)


def project(pieces, owners, weight, base, columns, so_far=None, dtype=jnp.bfloat16):
    rows, depth = pieces[0].shape
    count = len(pieces)
    width = min(512, columns)
    blocks = columns // width
    where = jnp.stack([jnp.asarray(w, jnp.int32) for w in (*owners, base)])
    in_specs = [pl.BlockSpec((rows, depth), lambda n, p, w: (0, 0))] * count
    in_specs.append(pl.BlockSpec((depth, width), lambda n, p, w: (w[p], w[count] * blocks + n)))
    operands = [*pieces, weight]
    if so_far is not None:
        in_specs.append(pl.BlockSpec((rows, width), lambda n, p, w: (0, n)))
        operands.append(so_far)
    return pl.pallas_call(
        functools.partial(project_kernel, count, so_far is not None),
        grid_spec=pltpu.PrefetchScalarGridSpec(
            num_scalar_prefetch=1,
            grid=(blocks, count),
            in_specs=in_specs,
            out_specs=pl.BlockSpec((rows, width), lambda n, p, w: (0, n)),
            scratch_shapes=[pltpu.VMEM((rows, width), jnp.float32)],
        ),
        out_shape=jax.ShapeDtypeStruct((rows, columns), dtype),
        compiler_params=pltpu.CompilerParams(vmem_limit_bytes=40 * MIB),
        cost_estimate=pl.CostEstimate(
            flops=2 * rows * depth * count * columns,
            bytes_accessed=2 * depth * count * (columns + rows) + 4 * rows * columns,
            transcendentals=0,
        ),
    )(where, *operands)


def exchange_sum(part, size):
    if size != 4:
        return lax.psum(part, "tp").astype(jnp.float32)
    total = part.astype(jnp.float32)
    for shift in (1, 2, 3):
        total = total + lax.ppermute(
            part, "tp", [(t, (t + shift) % size) for t in range(size)]
        ).astype(jnp.float32)
    return total


def relay(own, size):
    right = left = own
    rights, lefts = [], []
    for step in range(1, size):
        right = lax.ppermute(right, "tp", [(t, t + 1) for t in range(step - 1, size - 1)])
        left = lax.ppermute(left, "tp", [(t, t - 1) for t in range(1, size - step + 1)])
        rights.append(right)
        lefts.append(left)
    me = lax.axis_index("tp")
    found = [
        jnp.where(me >= k, rights[k - 1], lefts[size - k - 1]) for k in range(1, size)
    ]
    return found, rights, lefts


def body(
    x_attn,
    w_query,
    w_keyval,
    cache_pool,
    page_table,
    cached_len,
    page_dest,
    mamba_in,
    gate_in,
    conv_prev,
    state_prev,
    conv_weight,
    conv_bias,
    w_xdt,
    w_bc,
    w_dt,
    dt_bias,
    a_log,
    d_skip,
):
    tp_size = lax.axis_size("tp")
    tp_index = lax.axis_index("tp")
    token_count = x_attn.shape[0]
    own_heads = w_query.shape[1] // HEAD_DIM
    group_size = HEADS // KV_HEADS
    own_groups = max(1, own_heads // group_size)
    per_group = own_heads // own_groups
    head_cols = 2 * HEAD_DIM
    kv_cols = w_keyval.shape[1]
    slice_cols = kv_cols // tp_size
    first_group = tp_index * own_heads // group_size

    line = tp_size == 4
    if line:
        others, rights, lefts = relay(x_attn, tp_size)

    extended = jnp.concatenate([conv_prev[0], mamba_in], axis=0).astype(jnp.float32)
    convolved = jnp.broadcast_to(conv_bias[None, :], mamba_in.shape)
    for offset in range(conv_weight.shape[0]):
        convolved = (
            convolved + conv_weight[offset][None, :] * extended[offset : offset + token_count]
        )
    xconv = jax.nn.silu(convolved).astype(jnp.bfloat16)
    proj_part = jnp.dot(xconv, w_xdt, preferred_element_type=jnp.float32)
    select_part = jnp.dot(xconv, w_bc, preferred_element_type=jnp.float32)
    rank = w_xdt.shape[1]
    parts = jnp.concatenate([proj_part, select_part], axis=1).astype(jnp.bfloat16)
    if line:
        parts, _, _ = lax.optimization_barrier((parts, rights[0], lefts[0]))
    summed = exchange_sum(parts, tp_size)
    projected, selection = summed[:, :rank], summed[:, rank:]

    local_slots = cache_pool.shape[1]
    pool = cache_pool[0].reshape(local_slots * PAGE, KV_HEADS, head_cols)
    if own_heads >= group_size:
        outgoing_kv = pool.reshape(local_slots * PAGE, tp_size, own_groups * head_cols)
    else:
        outgoing_kv = jnp.repeat(pool, group_size // own_heads, axis=1)
    outgoing_kv = jnp.moveaxis(outgoing_kv, 1, 0)
    if line:
        outgoing_kv, _, _ = lax.optimization_barrier((outgoing_kv, rights[1], lefts[1]))
    cached = lax.all_to_all(outgoing_kv, "tp", split_axis=0, concat_axis=0, tiled=True)
    cached = cached.reshape(tp_size * local_slots * PAGE, own_groups * head_cols)
    usable = token_usable(page_table[0], jnp.arange(page_table.shape[1]), cached_len[0])
    bias = jnp.where(usable, 0.0, MASKED).astype(jnp.float32)[None, :]

    kv_own = own_groups * head_cols
    kv_base = first_group // own_groups
    if line:
        fresh_sum = project([x_attn], [tp_index], w_keyval, kv_base, kv_own, None, jnp.float32)
        query_sum = project([x_attn], [tp_index], w_query, 0, w_query.shape[1], None, jnp.float32)
        owners = [(tp_index + tp_size - k) % tp_size for k in range(1, tp_size)]
    else:
        fresh_sum = query_sum = None
        others = [lax.all_gather(x_attn, "tp", axis=1, tiled=True)]
        owners = [0]
    low_norm = (
        projected * lax.rsqrt(jnp.mean(projected * projected, axis=-1, keepdims=True) + 1e-06)
    ).astype(jnp.bfloat16)
    if line:
        low_norm, _, _ = lax.optimization_barrier((low_norm, rights[1], lefts[1]))
    mamba_out, last_state = scan(
        low_norm, selection, w_dt, dt_bias, xconv, gate_in, a_log, d_skip, state_prev[0]
    )

    fresh = project(others, owners, w_keyval, kv_base, kv_own, fresh_sum)
    queries = project(others, owners, w_query, 0, w_query.shape[1], query_sum)

    page_count = token_count // PAGE
    capacity = max(2, 2 * page_count // tp_size)
    target = page_dest[0, :, 0]
    page_ids = jnp.arange(page_count)
    earlier = (target[None, :] == target[:, None]) & (page_ids[None, :] < page_ids[:, None])
    ranking = jnp.sum(earlier.astype(jnp.int32), axis=1)
    slot_ids = jnp.arange(capacity)
    my_slice = lax.dynamic_slice_in_dim(
        fresh, tp_index * slice_cols - first_group * head_cols, slice_cols, 1
    )
    pieces_out = my_slice.reshape(page_count, PAGE * slice_cols)
    onehot = (
        (target[None, None, :] == jnp.arange(tp_size)[:, None, None])
        & (ranking[None, None, :] == slot_ids[None, :, None])
    ).astype(jnp.bfloat16)
    outgoing = jnp.einsum(
        "drj,jx->drx", onehot, pieces_out, preferred_element_type=jnp.float32
    ).astype(jnp.bfloat16)
    arrived = lax.all_to_all(outgoing, "tp", split_axis=0, concat_axis=2, tiled=True)
    decode = (
        arrived.reshape(capacity, tp_size, PAGE, slice_cols)
        .transpose(0, 2, 1, 3)
        .reshape(1, capacity, PAGE, kv_cols)
    )
    attn_out = attend(queries, cached, fresh, bias, own_groups, per_group)
    return (attn_out, decode, mamba_out, last_state[None])


def solution(mesh):
    return jax.shard_map(
        body,
        mesh=mesh,
        in_specs=(
            P(("grp", "pd"), "tp"),
            P(None, "tp"),
            P(),
            P(("grp", "pd"), "tp", None, None),
            P(("grp", "pd"), None),
            P(("grp", "pd")),
            P(("grp", "pd"), None, None),
            P(("grp", "pd"), "tp"),
            P(("grp", "pd"), "tp"),
            P(("grp", "pd"), None, "tp"),
            P(("grp", "pd"), None, "tp"),
            P(None, "tp"),
            P("tp"),
            P("tp", None),
            P("tp", None),
            P(None, "tp"),
            P("tp"),
            P(None, "tp"),
            P("tp"),
        ),
        out_specs=(
            P(("grp", "pd"), "tp"),
            P(("grp", "pd"), "tp", None, None),
            P(("grp", "pd"), "tp"),
            P(("grp", "pd"), None, "tp"),
        ),
        check_vma=False,
    )
```

```python
import functools
import math

import jax
import jax.numpy as jnp
from jax import lax
from jax.experimental import pallas as pl
from jax.experimental.pallas import tpu as pltpu
from jax.sharding import PartitionSpec as P

HEADS = 64
KV_HEADS = 8
HEAD_DIM = 128
PAGE = 16
MASKED = -1e30
LOG2E = math.log2(math.e)
MIB = 1024 * 1024


def token_usable(page_map, slot_ids, length):
    logical = jnp.sum(
        jnp.where(
            page_map[None, :] == slot_ids[:, None], jnp.arange(page_map.shape[0])[None, :], 0
        ),
        axis=1,
    )
    positions = logical[:, None] * PAGE + jnp.arange(PAGE)[None, :]
    return (positions < length).reshape(-1)


def attention_kernel(chunk, bias_ref, query_ref, cached_ref, fresh_ref, out_ref):
    tokens = query_ref.shape[0]
    query = query_ref[...]
    scale = LOG2E / math.sqrt(HEAD_DIM)
    contract = (((1,), (1,)), ((), ()))

    def scored(keys):
        return lax.dot_general(query, keys, contract, preferred_element_type=jnp.float32) * scale

    rows = lax.broadcasted_iota(jnp.int32, (tokens, tokens), 0)
    cols = lax.broadcasted_iota(jnp.int32, (tokens, tokens), 1)
    near = jnp.where(rows >= cols, scored(fresh_ref[:, :HEAD_DIM]), MASKED)
    near_high = jnp.max(near, axis=1, keepdims=True)

    def mix(weights, values):
        return jnp.dot(
            weights.astype(jnp.bfloat16), values, preferred_element_type=jnp.float32
        )

    chunks = cached_ref.shape[0] // chunk
    if chunks == 1:
        far = scored(cached_ref[:, :HEAD_DIM]) + bias_ref[...]
        high = jnp.maximum(near_high, jnp.max(far, axis=1, keepdims=True))
        near_w = jnp.exp2(near - high)
        far_w = jnp.exp2(far - high)
        total = jnp.sum(near_w, axis=1, keepdims=True) + jnp.sum(far_w, axis=1, keepdims=True)
        mixture = mix(near_w, fresh_ref[:, HEAD_DIM:]) + mix(far_w, cached_ref[:, HEAD_DIM:])
        out_ref[...] = (mixture / total).astype(out_ref.dtype)
        return
    near_w = jnp.exp2(near - near_high)
    start = (
        near_high,
        jnp.sum(near_w, axis=1, keepdims=True),
        mix(near_w, fresh_ref[:, HEAD_DIM:]),
    )

    def step(i, carry):
        high, total, mixture = carry
        here = pl.ds(pl.multiple_of(i * chunk, chunk), chunk)
        far = scored(cached_ref[here, :HEAD_DIM]) + bias_ref[:, here]
        peak = jnp.maximum(high, jnp.max(far, axis=1, keepdims=True))
        far_w = jnp.exp2(far - peak)
        shrink = jnp.exp2(high - peak)
        return (
            peak,
            total * shrink + jnp.sum(far_w, axis=1, keepdims=True),
            mixture * shrink + mix(far_w, cached_ref[here, HEAD_DIM:]),
        )

    _, total, mixture = lax.fori_loop(0, chunks, step, start)
    out_ref[...] = (mixture / total).astype(out_ref.dtype)


def attend(queries, cached, fresh, bias, own_groups, per_group):
    tokens = queries.shape[0]
    length = cached.shape[0]
    chunk = min(1024, length)
    return pl.pallas_call(
        functools.partial(attention_kernel, chunk),
        grid=(own_groups, per_group),
        out_shape=jax.ShapeDtypeStruct(queries.shape, jnp.bfloat16),
        in_specs=[
            pl.BlockSpec((1, length), lambda g, h: (0, 0)),
            pl.BlockSpec((tokens, HEAD_DIM), lambda g, h: (0, g * per_group + h)),
            pl.BlockSpec((length, 2 * HEAD_DIM), lambda g, h: (0, g)),
            pl.BlockSpec((tokens, 2 * HEAD_DIM), lambda g, h: (0, g)),
        ],
        out_specs=pl.BlockSpec((tokens, HEAD_DIM), lambda g, h: (0, g * per_group + h)),
        compiler_params=pltpu.CompilerParams(vmem_limit_bytes=40 * MIB),
        cost_estimate=pl.CostEstimate(
            flops=4 * tokens * queries.shape[1] * (length + tokens),
            bytes_accessed=4 * queries.size + 2 * cached.size,
            transcendentals=tokens * own_groups * per_group * (length + tokens),
        ),
    )(bias, queries, cached, fresh)


def scan_kernel(count, *refs):
    norm_ref, spread_ref, wdt_ref, bias_ref, xconv_ref = refs[:5]
    gate_ref, alog_ref, skip_ref, init_ref = refs[5:count]
    out_ref, final_ref, step_s, push_s, read_s = refs[-5:]
    tokens, width = xconv_ref.shape
    states = alog_ref.shape[0]
    raw = jnp.dot(norm_ref[...], wdt_ref[...], preferred_element_type=jnp.float32) + bias_ref[...]
    step_size = jnp.maximum(raw, 0.0) + jnp.log1p(jnp.exp(-jnp.abs(raw)))
    step_s[...] = step_size
    push_s[...] = step_size * xconv_ref[...].astype(jnp.float32)
    rate = jnp.exp(alog_ref[...]) * (-LOG2E)
    unroll = 8

    def some(block, state):
        base = pl.multiple_of(block * unroll, unroll)
        for i in range(unroll):
            here = pl.ds(base + i, 1)
            step_row = jnp.broadcast_to(step_s[here, :], (states, width))
            push_row = jnp.broadcast_to(push_s[here, :], (states, width))
            columns = spread_ref[base + i]
            into = jnp.concatenate([columns[:states]] * (width // 128), axis=1)
            outof = jnp.concatenate([columns[states:]] * (width // 128), axis=1)
            state = jnp.exp2(step_row * rate) * state + push_row * into
            read_s[here, :] = jnp.sum(outof * state, axis=0, keepdims=True)
        return state

    final_ref[...] = lax.fori_loop(0, tokens // unroll, some, init_ref[...])
    readout = read_s[...] + skip_ref[...] * xconv_ref[...].astype(jnp.float32)
    gate = gate_ref[...].astype(jnp.float32)
    out_ref[...] = (readout * (gate * jax.nn.sigmoid(gate))).astype(out_ref.dtype)


def scan(low_norm, selection, w_dt, dt_bias, xconv, gate, a_log, d_skip, initial, late):
    tokens, channels = xconv.shape
    rank = low_norm.shape[1]
    states = a_log.shape[0]
    width = min(512, channels)
    spread = jnp.broadcast_to(selection[:, :, None], (tokens, 2 * states, 128))
    calls = 4 if channels // width >= 4 else 1
    blocks = channels // width // calls
    results = None
    for call in range(calls):

        def whole(shape):
            return pl.BlockSpec(shape, lambda c: (0,) * len(shape))

        def columns(rows, first=call * blocks):
            return pl.BlockSpec((rows, width), lambda c: (0, first + c))

        operands = [
            late if call == 3 else low_norm, spread, w_dt, dt_bias[None, :], xconv, gate, a_log, d_skip[None, :], initial
        ]
        in_specs = [
            whole((tokens, rank)),
            whole((tokens, 2 * states, 128)),
            columns(rank),
            columns(1),
            columns(tokens),
            columns(tokens),
            columns(states),
            columns(1),
            columns(states),
        ]
        aliases = {}
        if results is not None:
            aliases = {len(operands): 0, len(operands) + 1: 1}
            operands += results
            in_specs += [pl.BlockSpec(memory_space=pl.ANY)] * 2
        results = pl.pallas_call(
            functools.partial(scan_kernel, 9),
            grid=(blocks,),
            out_shape=(
                jax.ShapeDtypeStruct((tokens, channels), jnp.bfloat16),
                jax.ShapeDtypeStruct((states, channels), jnp.float32),
            ),
            in_specs=in_specs,
            out_specs=(columns(tokens), columns(states)),
            scratch_shapes=[pltpu.VMEM((tokens, width), jnp.float32)] * 3,
            input_output_aliases=aliases,
            compiler_params=pltpu.CompilerParams(vmem_limit_bytes=40 * MIB),
            cost_estimate=pl.CostEstimate(
                flops=2 * tokens * channels * rank // calls,
                bytes_accessed=60 * MIB // calls,
                transcendentals=tokens * channels * states // calls,
            ),
        )(*operands)
    return results


def project_kernel(count, has_sum, where_ref, *refs):
    pieces, weight_ref = refs[:count], refs[count]
    out_ref, total = refs[-2], refs[-1]
    at = pl.program_id(1)

    @pl.when(at == 0)
    def _():
        total[...] = refs[count + 1][...] if has_sum else jnp.zeros_like(total)

    for i in range(count):

        @pl.when(at == i)
        def _(i=i):
            total[...] += jnp.dot(
                pieces[i][...], weight_ref[...], preferred_element_type=jnp.float32
            )

    @pl.when(at == count - 1)
    def _():
        out_ref[...] = total[...].astype(out_ref.dtype)


def project(pieces, owners, weight, base, columns, so_far=None, dtype=jnp.bfloat16):
    rows, depth = pieces[0].shape
    count = len(pieces)
    width = min(512, columns)
    blocks = columns // width
    where = jnp.stack([jnp.asarray(w, jnp.int32) for w in (*owners, base)])
    in_specs = [pl.BlockSpec((rows, depth), lambda n, p, w: (0, 0))] * count
    in_specs.append(pl.BlockSpec((depth, width), lambda n, p, w: (w[p], w[count] * blocks + n)))
    operands = [*pieces, weight]
    if so_far is not None:
        in_specs.append(pl.BlockSpec((rows, width), lambda n, p, w: (0, n)))
        operands.append(so_far)
    return pl.pallas_call(
        functools.partial(project_kernel, count, so_far is not None),
        grid_spec=pltpu.PrefetchScalarGridSpec(
            num_scalar_prefetch=1,
            grid=(blocks, count),
            in_specs=in_specs,
            out_specs=pl.BlockSpec((rows, width), lambda n, p, w: (0, n)),
            scratch_shapes=[pltpu.VMEM((rows, width), jnp.float32)],
        ),
        out_shape=jax.ShapeDtypeStruct((rows, columns), dtype),
        compiler_params=pltpu.CompilerParams(vmem_limit_bytes=40 * MIB),
        cost_estimate=pl.CostEstimate(
            flops=2 * rows * depth * count * columns,
            bytes_accessed=2 * depth * count * (columns + rows) + 4 * rows * columns,
            transcendentals=0,
        ),
    )(where, *operands)


def exchange_sum(part, size):
    if size != 4:
        return lax.psum(part, "tp").astype(jnp.float32)
    total = part.astype(jnp.float32)
    for shift in (1, 2, 3):
        total = total + lax.ppermute(
            part, "tp", [(t, (t + shift) % size) for t in range(size)]
        ).astype(jnp.float32)
    return total


def pass_on(right, left, step, size):
    return (
        lax.ppermute(right, "tp", [(t, t + 1) for t in range(step - 1, size - 1)]),
        lax.ppermute(left, "tp", [(t, t - 1) for t in range(1, size - step + 1)]),
    )


def body(
    x_attn,
    w_query,
    w_keyval,
    cache_pool,
    page_table,
    cached_len,
    page_dest,
    mamba_in,
    gate_in,
    conv_prev,
    state_prev,
    conv_weight,
    conv_bias,
    w_xdt,
    w_bc,
    w_dt,
    dt_bias,
    a_log,
    d_skip,
):
    tp_size = lax.axis_size("tp")
    tp_index = lax.axis_index("tp")
    token_count = x_attn.shape[0]
    own_heads = w_query.shape[1] // HEAD_DIM
    group_size = HEADS // KV_HEADS
    own_groups = max(1, own_heads // group_size)
    per_group = own_heads // own_groups
    head_cols = 2 * HEAD_DIM
    kv_cols = w_keyval.shape[1]
    slice_cols = kv_cols // tp_size
    first_group = tp_index * own_heads // group_size

    line = tp_size == 4
    if line:
        first = pass_on(x_attn, x_attn, 1, tp_size)

    extended = jnp.concatenate([conv_prev[0], mamba_in], axis=0).astype(jnp.float32)
    convolved = jnp.broadcast_to(conv_bias[None, :], mamba_in.shape)
    for offset in range(conv_weight.shape[0]):
        convolved = (
            convolved + conv_weight[offset][None, :] * extended[offset : offset + token_count]
        )
    xconv = jax.nn.silu(convolved).astype(jnp.bfloat16)
    proj_part = jnp.dot(xconv, w_xdt, preferred_element_type=jnp.float32)
    select_part = jnp.dot(xconv, w_bc, preferred_element_type=jnp.float32)
    rank = w_xdt.shape[1]
    parts = jnp.concatenate([proj_part, select_part], axis=1).astype(jnp.bfloat16)
    summed = exchange_sum(parts, tp_size)
    if line:
        *begun, summed = lax.optimization_barrier((*first, summed))
        second = pass_on(*begun, 2, tp_size)
    projected, selection = summed[:, :rank], summed[:, rank:]

    local_slots = cache_pool.shape[1]
    pool = cache_pool[0].reshape(local_slots * PAGE, KV_HEADS, head_cols)
    if own_heads >= group_size:
        outgoing_kv = pool.reshape(local_slots * PAGE, tp_size, own_groups * head_cols)
    else:
        outgoing_kv = jnp.repeat(pool, group_size // own_heads, axis=1)
    outgoing_kv = jnp.moveaxis(outgoing_kv, 1, 0)
    if line:
        outgoing_kv, _, _ = lax.optimization_barrier((outgoing_kv, *second))
    cached = lax.all_to_all(outgoing_kv, "tp", split_axis=0, concat_axis=0, tiled=True)
    cached = cached.reshape(tp_size * local_slots * PAGE, own_groups * head_cols)
    usable = token_usable(page_table[0], jnp.arange(page_table.shape[1]), cached_len[0])
    bias = jnp.where(usable, 0.0, MASKED).astype(jnp.float32)[None, :]

    kv_own = own_groups * head_cols
    kv_base = first_group // own_groups
    if line:
        fresh_sum = project([x_attn], [tp_index], w_keyval, kv_base, kv_own, None, jnp.float32)
        query_sum = project([x_attn], [tp_index], w_query, 0, w_query.shape[1], None, jnp.float32)
    else:
        fresh_sum = query_sum = None
        others = [lax.all_gather(x_attn, "tp", axis=1, tiled=True)]
        owners = [0]
    low_norm = (
        projected * lax.rsqrt(jnp.mean(projected * projected, axis=-1, keepdims=True) + 1e-06)
    ).astype(jnp.bfloat16)
    if line:
        late, *more = lax.optimization_barrier((low_norm, *second))
        third = pass_on(*more, 3, tp_size)
    else:
        late = low_norm
    mamba_out, last_state = scan(
        low_norm, selection, w_dt, dt_bias, xconv, gate_in, a_log, d_skip, state_prev[0], late
    )

    if line:
        blocks = (first, second, third)
        others = [
            jnp.where(tp_index >= k, blocks[k - 1][0], blocks[tp_size - k - 1][1])
            for k in (2, 1, 3)
        ]
        owners = [(tp_index + tp_size - k) % tp_size for k in (2, 1, 3)]
        fresh_sum = project(
            others[:1], owners[:1], w_keyval, kv_base, kv_own, fresh_sum, jnp.float32
        )
        query_sum = project(
            others[:1], owners[:1], w_query, 0, w_query.shape[1], query_sum, jnp.float32
        )
        others, owners = others[1:], owners[1:]
    fresh = project(others, owners, w_keyval, kv_base, kv_own, fresh_sum)
    queries = project(others, owners, w_query, 0, w_query.shape[1], query_sum)

    page_count = token_count // PAGE
    capacity = max(2, 2 * page_count // tp_size)
    target = page_dest[0, :, 0]
    page_ids = jnp.arange(page_count)
    earlier = (target[None, :] == target[:, None]) & (page_ids[None, :] < page_ids[:, None])
    ranking = jnp.sum(earlier.astype(jnp.int32), axis=1)
    slot_ids = jnp.arange(capacity)
    my_slice = lax.dynamic_slice_in_dim(
        fresh, tp_index * slice_cols - first_group * head_cols, slice_cols, 1
    )
    pieces_out = my_slice.reshape(page_count, PAGE * slice_cols)
    onehot = (
        (target[None, None, :] == jnp.arange(tp_size)[:, None, None])
        & (ranking[None, None, :] == slot_ids[None, :, None])
    ).astype(jnp.bfloat16)
    outgoing = jnp.einsum(
        "drj,jx->drx", onehot, pieces_out, preferred_element_type=jnp.float32
    ).astype(jnp.bfloat16)
    arrived = lax.all_to_all(outgoing, "tp", split_axis=0, concat_axis=2, tiled=True)
    decode = (
        arrived.reshape(capacity, tp_size, PAGE, slice_cols)
        .transpose(0, 2, 1, 3)
        .reshape(1, capacity, PAGE, kv_cols)
    )
    attn_out = attend(queries, cached, fresh, bias, own_groups, per_group)
    return (attn_out, decode, mamba_out, last_state[None])


def solution(mesh):
    return jax.shard_map(
        body,
        mesh=mesh,
        in_specs=(
            P(("grp", "pd"), "tp"),
            P(None, "tp"),
            P(),
            P(("grp", "pd"), "tp", None, None),
            P(("grp", "pd"), None),
            P(("grp", "pd")),
            P(("grp", "pd"), None, None),
            P(("grp", "pd"), "tp"),
            P(("grp", "pd"), "tp"),
            P(("grp", "pd"), None, "tp"),
            P(("grp", "pd"), None, "tp"),
            P(None, "tp"),
            P("tp"),
            P("tp", None),
            P("tp", None),
            P(None, "tp"),
            P("tp"),
            P(None, "tp"),
            P("tp"),
        ),
        out_specs=(
            P(("grp", "pd"), "tp"),
            P(("grp", "pd"), "tp", None, None),
            P(("grp", "pd"), "tp"),
            P(("grp", "pd"), None, "tp"),
        ),
        check_vma=False,
    )
```
